128 devices in a mesh: mem: 8 (over z, core), col: 16 (over x, y).
Axes of the slice: x: 4, y: 4, z: 4, core: 2. Of those that a mesh axis runs over, the one named last changes fastest.
Arguments:
- prior_trajectory: bfloat16 [94, 1024, 1024], P(None, 'col', 'mem'), may hold values from -6 to 6
- predicted_measurements: bfloat16 [4096, 128, 1024], P('col', None, 'mem'), may hold values from -6 to 6
- departure_vector: float32 [4096, 128], replicated, may hold values from -6 to 6
- measurement_error_spread: float32 [4096, 128], replicated, may hold values from 0.01 to 1
- valid_tallies: int32 [4096], replicated, may hold values from 1 to 128
- area_point_sequence: int32 [1024], P('col'), may hold values from 0 to 63, as said below
- nearby_batch_map: int32 [128, 3, 3], replicated, may hold values from 0 to 255, as said below
Outputs:
- analysis: bfloat16 [94, 1024, 1024], P(None, ('mem', 'col'))
The draws below stay inside these ranges and needn't reach their ends.
Inputs may be any that keep to these rules, and one draw needn't show every extreme that they name: `area_point_sequence`: each aligned block of 64 entries, one region's, holds every number 0 to 63 once. `nearby_batch_map`: the 3 entries of one group and slot are different.
All inputs are finite; a program needn't handle non-finite values.
Results may differ from the reference program's by a relative error of at most 0.009.
The reference program's roundings to bfloat16 on the way count: a program that leaves them out, or rounds other values in their place, can miss the bound.
Values may be sent and summed in bfloat16 or wider, within the bound.
A program may use at most 128 MiB of HBM per device.

```python
import math
import jax
import jax.numpy as jnp
from jax import lax

MEMBER_COUNT_K = 1024
HEIGHT_LAYERS = 94
BLK = 128
NPER = 3
NS_ITERS = 5
CD = 8
OBR = 256
SLAB = 64
GRID_POINT_COUNT = 1024
NBLK = 4096
GROUPS = 128
N_COL = 16


def draw_area_point_sequence(key, part):
    key = jax.random.fold_in(key, 11)
    subkeys = jax.random.split(key, GRID_POINT_COUNT // SLAB)
    perms = jax.vmap(lambda subkey: jax.random.permutation(subkey, SLAB))(subkeys)
    return perms.reshape(-1).astype(jnp.int32)


def draw_nearby_batch_map(key, part):
    key = jax.random.fold_in(key, 23)
    subkeys = jax.random.split(key, GROUPS * 3)
    picks = jax.vmap(lambda subkey: jax.random.permutation(subkey, OBR)[:NPER])(subkeys)
    return picks.reshape(GROUPS, 3, NPER).astype(jnp.int32)


def touch_ends(entries, stream_key, low, largest):
    extent = entries.shape
    spot = [jax.random.randint(jax.random.fold_in(stream_key, axis), (), 0, extent[axis]) for axis in range(len(extent))]
    entries = entries.at[tuple(spot)].set(low)
    longest = extent.index(max(extent))
    spot[longest] = (spot[longest] + 1) % extent[longest]
    return entries.at[tuple(spot)].set(largest)


def level_of(key, extent, cuts, smallest, largest):
    factor_of, own = 1.0, jax.random.fold_in(key, 6)
    for position, shards_of in cuts:
        steps = jnp.exp(jax.random.uniform(jax.random.fold_in(own, position), (shards_of,), jnp.float32, smallest / len(cuts), largest / len(cuts)))
        factor_of = factor_of * jnp.repeat(steps, extent[position] // shards_of).reshape([-1 if axis == position else 1 for axis in range(len(extent))])
    return factor_of


def bell_draw(key, dims, deviation, reach, pieces=(), kind=jnp.bfloat16):
    gain = level_of(key, dims, pieces, -0.22, 0.18) if pieces else 1.0
    array = jax.random.normal(key, dims, jnp.float32) * deviation * gain
    return jnp.minimum(jnp.maximum(array, -reach), reach).astype(kind)


def setup_inputs(seed: int = 0) -> dict:
    streams_of = jax.random.split(jax.random.key(seed), 8)
    return {
        "prior_trajectory": bell_draw(streams_of[0], (HEIGHT_LAYERS, GRID_POINT_COUNT, MEMBER_COUNT_K), 1.0, 6.0, ((1, 16), (2, 8))),
        "predicted_measurements": bell_draw(streams_of[1], (NBLK, BLK, MEMBER_COUNT_K), 1.0, 6.0, ((0, 16), (2, 8))),
        "departure_vector": bell_draw(streams_of[2], (NBLK, BLK), 1.0, 6.0, (), jnp.float32),
        "measurement_error_spread": jnp.clip(jnp.exp(jax.random.uniform(streams_of[3], (NBLK, BLK), jnp.float32, math.log(0.01), math.log(1.0))), 0.01, 1.0),
        "valid_tallies": touch_ends(jax.random.randint(streams_of[4], (NBLK,), 1, BLK + 1), jax.random.fold_in(streams_of[4], 1), 1, BLK).astype(jnp.int32),
        "area_point_sequence": draw_area_point_sequence(jax.random.fold_in(streams_of[7], 71), 0),
        "nearby_batch_map": draw_nearby_batch_map(jax.random.fold_in(streams_of[7], 71), 0),
    }


def analyse(model_quantities, obs_rows, innov_rows, var_rows, count_rows):
    members = obs_rows.shape[1]
    slots = innov_rows.shape[1]
    valid_mask = (jnp.arange(slots, dtype=jnp.int32)[None, :] < count_rows[:, None]).astype(jnp.float32)
    root_w = (valid_mask * lax.rsqrt(var_rows)).reshape(-1, 1)
    obs_mean = lax.optimization_barrier(jnp.sum(obs_rows, axis=1, dtype=jnp.float32, keepdims=True)) / members
    scaled = ((obs_rows - obs_mean) * root_w).astype(jnp.bfloat16)
    cross = lax.dot_general(scaled, scaled, (((0,), (0,)), ((), ())), preferred_element_type=jnp.float32)
    identity = jnp.eye(members, dtype=jnp.float32)
    system = cross + (members - 1.0) * identity
    bound = members - 1.0 + jnp.sqrt(jnp.sum(cross * cross))
    drive_vec = (innov_rows.reshape(-1, 1) * root_w).astype(jnp.bfloat16)
    projected = lax.dot_general(scaled, drive_vec, (((0,), (0,)), ((), ())), preferred_element_type=jnp.float32)[:, 0]
    root_iter = (system / bound).astype(jnp.bfloat16)
    inverse = root_iter
    for sweep in range(NS_ITERS):
        if sweep == 0:
            factor = ((3.0 * identity - root_iter) * 0.5).astype(jnp.bfloat16)
            inverse = factor
        else:
            product = jnp.dot(inverse, root_iter, preferred_element_type=jnp.float32)
            factor = ((3.0 * identity - product) * 0.5).astype(jnp.bfloat16)
            inverse = jnp.dot(factor, inverse, preferred_element_type=jnp.float32).astype(jnp.bfloat16)
        if sweep + 1 < NS_ITERS:
            root_iter = jnp.dot(root_iter, factor, preferred_element_type=jnp.float32).astype(jnp.bfloat16)
    inverse_f = inverse.astype(jnp.float32)
    half_step = jnp.dot(inverse_f, projected, precision=lax.Precision.HIGHEST)
    mean_w = jnp.dot(inverse_f, half_step, precision=lax.Precision.HIGHEST) / bound
    weights = (jnp.sqrt((members - 1.0) / bound) * inverse_f + mean_w[:, None]).astype(jnp.bfloat16)
    layer_indices = model_quantities.shape[0]
    group_column_list = model_quantities.shape[1]
    flat_state = model_quantities.reshape(layer_indices * group_column_list, members)
    state_mean = lax.optimization_barrier(jnp.sum(flat_state, axis=1, dtype=jnp.float32, keepdims=True)) / members
    spread = (flat_state - state_mean).astype(jnp.bfloat16)
    result = state_mean + jnp.dot(spread, weights, preferred_element_type=jnp.float32)
    return result.astype(jnp.bfloat16).reshape(layer_indices, group_column_list, members)

def reference(prior_trajectory, predicted_measurements, departure_vector, measurement_error_spread, valid_tallies, area_point_sequence, nearby_batch_map):

    def one_group(group_id):
        mem_index = group_id // N_COL
        col_index = group_id % N_COL
        start = (col_index * SLAB + mem_index * CD).astype(jnp.int32)
        local_cols = lax.dynamic_slice_in_dim(area_point_sequence, start, CD)
        point_indices = (local_cols + col_index * SLAB).astype(jnp.int32)
        model_quantities = jnp.take(prior_trajectory, point_indices, axis=1)
        pattern = nearby_batch_map[group_id]
        regions_of = (col_index + jnp.arange(3, dtype=jnp.int32) - 1 + N_COL) % N_COL
        blocks = (regions_of[:, None] * OBR + pattern).reshape(-1).astype(jnp.int32)
        obs_rows = jnp.take(predicted_measurements, blocks, axis=0).reshape(-1, MEMBER_COUNT_K)
        return analyse(model_quantities, obs_rows, jnp.take(departure_vector, blocks, axis=0), jnp.take(measurement_error_spread, blocks, axis=0), jnp.take(valid_tallies, blocks, axis=0))
    results = lax.map(one_group, jnp.arange(GROUPS, dtype=jnp.int32))
    return jnp.moveaxis(results, 0, 1).reshape(HEIGHT_LAYERS, GRID_POINT_COUNT, MEMBER_COUNT_K)
```

```python
import jax
import jax.numpy as jnp
from jax import lax
from jax.experimental import pallas as pl
from jax.experimental.pallas import tpu as pltpu
from jax.sharding import PartitionSpec as P

NS_ITERS = 5
N_MEM, N_COL = 8, 16
K = 1024
LAYERS, CD, SLAB = 94, 8, 64
STATE_ROWS = LAYERS * CD
OBR, BLK, NPER = 256, 128, 3
SLOT_ROWS = NPER * BLK
OBS_ROWS = 3 * SLOT_ROWS
LANES = K // N_MEM
B = 256
NB = K // B
LOADS = 8
STATE_CUTS = (0, 256, 512, 752)
MESH = pl.DeviceIdType.MESH
f32, bf16 = jnp.float32, jnp.bfloat16


def unit_block():
    row = lax.broadcasted_iota(jnp.int32, (B, B), 0)
    column = lax.broadcasted_iota(jnp.int32, (B, B), 1)
    return jnp.where(row == column, 1.0, 0.0).astype(f32)


def span(i):
    return slice(i * B, (i + 1) * B)


def put_pair(dst, i, j, tile):
    dst[span(i), span(j)] = tile
    if i != j:
        dst[span(j), span(i)] = tile.T


def halved(tile, diagonal):
    return (3.0 * unit_block() - tile) * 0.5 if diagonal else tile * -0.5


def symmetric_dot(a, b, dst, as_factor=False):
    for j in range(NB):
        for i in range(j + 1):
            tile = jnp.dot(a[span(i), :], b[:, span(j)], preferred_element_type=f32)
            if as_factor:
                tile = halved(tile, i == j)
            put_pair(dst, i, j, tile.astype(bf16))


def precise_row_times(row, matrix):
    high = row.astype(bf16).astype(f32)
    middle = (row - high).astype(bf16).astype(f32)
    low = row - high - middle
    place = lax.broadcasted_iota(jnp.int32, row.shape, 0)
    terms = jnp.where(place == 0, high, jnp.where(place == 1, middle, jnp.where(place == 2, low, 0.0)))
    product = jnp.dot(terms.astype(bf16), matrix[...], preferred_element_type=f32)
    return jnp.broadcast_to(jnp.sum(product, axis=0, keepdims=True), product.shape)


def kernel(
    prior_hbm, obs_hbm, departure_hbm, variance_hbm, counts, sequence, nearby, out_hbm,
    prior, obs, departure, variance, outgoing, rows, states_out, states, scaled, scaled_t,
    cross, root_a, root_b, inverse_a, inverse_b, factor, spread, result, pick, drive,
    load_sem, obs_send, obs_recv, state_send, state_recv, out_sem,
):
    m = lax.axis_index("mem")
    c = lax.axis_index("col")

    def column_of(s):
        return lax.rem(c - s + 1 + N_COL, N_COL)

    def member(dz, dk):
        return lax.rem(m // 2 + dz, 4) * 2 + lax.rem(lax.rem(m, 2) + dk, 2)

    hops = [(dz, dk) for dz in (1, 3, 2, 0) for dk in (0, 1)]
    partners = [(s, dz, dk) for s in (1, 0, 2) for dz, dk in hops if (s, dz, dk) != (1, 0, 0)]

    barrier = pltpu.get_barrier_semaphore()
    for s, dz, dk in partners:
        pl.semaphore_signal(
            barrier, inc=1, device_id={"mem": member(dz, dk), "col": column_of(s)}, device_id_type=MESH
        )

    loads = []
    part = OBR // LOADS
    for i in range(LOADS):
        cut = pl.ds(i * part, part)
        loads.append(pltpu.make_async_copy(obs_hbm.at[cut], obs.at[cut], load_sem.at[i]))
    for s in range(3):
        region = lax.rem(c + s - 1 + N_COL, N_COL)
        cut = pl.ds(pl.multiple_of(region * OBR, OBR), OBR)
        loads.append(pltpu.make_async_copy(departure_hbm.at[cut], departure.at[s], load_sem.at[LOADS + 2 * s]))
        loads.append(pltpu.make_async_copy(variance_hbm.at[cut], variance.at[s], load_sem.at[LOADS + 2 * s + 1]))
    loads.append(pltpu.make_async_copy(prior_hbm, prior, load_sem.at[LOADS + 6]))
    for copy in loads:
        copy.start()
    for copy in loads[:LOADS]:
        copy.wait()

    def block_index(group_m, group_c, s, k):
        return nearby[s, k, group_m * N_COL + group_c]

    for k in range(NPER):
        at = SLOT_ROWS + k * BLK
        rows[m, at : at + BLK, :] = obs[block_index(m, c, 1, k)]
    pl.semaphore_wait(barrier, len(partners))
    obs_copies = []
    for n, (s, dz, dk) in enumerate(partners):
        to_m, to_c = member(dz, dk), column_of(s)
        for k in range(NPER):
            outgoing[n, k * BLK : (k + 1) * BLK, :] = obs[block_index(to_m, to_c, s, k)]
        copy = pltpu.make_async_remote_copy(
            src_ref=outgoing.at[n],
            dst_ref=rows.at[m, pl.ds(s * SLOT_ROWS, SLOT_ROWS)],
            send_sem=obs_send.at[n],
            recv_sem=obs_recv.at[s * N_MEM + m],
            device_id={"mem": to_m, "col": to_c},
            device_id_type=MESH,
        )
        copy.start()
        obs_copies.append(copy)

    def wait_obs(s):
        for dz, dk in hops:
            if (s, dz, dk) != (1, 0, 0):
                source = member(dz, dk)
                pltpu.make_async_remote_copy(
                    src_ref=outgoing.at[0],
                    dst_ref=rows.at[source, pl.ds(s * SLOT_ROWS, SLOT_ROWS)],
                    send_sem=obs_send.at[0],
                    recv_sem=obs_recv.at[s * N_MEM + source],
                    device_id={"mem": source, "col": c},
                    device_id_type=MESH,
                ).wait_recv()

    for copy in loads[LOADS:]:
        copy.wait()
    place = lax.broadcasted_iota(jnp.int32, (1, 2 * SLAB), 1)
    for owner in range(N_MEM):
        for j in range(CD):
            column = sequence[owner * CD + j]
            for layer in range(2):
                r = owner * 2 * CD + layer * CD + j
                pick[r : r + 1, :] = jnp.where(place == column + layer * SLAB, 1.0, 0.0).astype(f32)
    picker = pick[...].astype(bf16)

    @pl.loop(0, LAYERS // 2)
    def _(p):
        pair = prior[pl.ds(p * 2, 2)].reshape(2 * SLAB, LANES)
        chosen = jnp.dot(picker, pair, preferred_element_type=f32).astype(bf16)
        at = pl.ds(pl.multiple_of(p * 2 * CD, 2 * CD), 2 * CD)
        for owner in range(N_MEM):
            states_out[owner, at, :] = chosen[owner * 2 * CD : (owner + 1) * 2 * CD]

    states[m] = states_out[m]

    lane = lax.broadcasted_iota(jnp.int32, (1, BLK), 1)

    def prepare(s):
        for k in range(NPER):
            at = s * SLOT_ROWS + k * BLK
            index = block_index(m, c, s, k)
            region = lax.rem(c + s - 1 + N_COL, N_COL)
            count = counts[region * OBR + index]
            row_w = jnp.where(lane < count, 1.0, 0.0) * lax.rsqrt(variance[s, pl.ds(index, 1), :])
            driven = (departure[s, pl.ds(index, 1), :] * row_w).astype(bf16)
            drive[:, at : at + BLK] = jnp.broadcast_to(driven, (16, BLK))
            column_w = jnp.broadcast_to(row_w, (BLK, BLK)).T
            total = rows[0, at : at + BLK, :].astype(f32)
            for source in range(1, N_MEM):
                total = total + rows[source, at : at + BLK, :].astype(f32)
            mean = jnp.sum(total, axis=1, keepdims=True) * (1.0 / K)
            for source in range(N_MEM):
                tile = ((rows[source, at : at + BLK, :].astype(f32) - mean) * column_w).astype(bf16)
                columns = slice(source * LANES, (source + 1) * LANES)
                scaled[at : at + BLK, columns] = tile
                scaled_t[columns, at : at + BLK] = tile.T

    early, late = slice(0, 2 * SLOT_ROWS), slice(2 * SLOT_ROWS, OBS_ROWS)
    wait_obs(1)
    prepare(1)
    wait_obs(0)
    prepare(0)
    for j in range(NB):
        for i in range(j + 1):
            cross[span(i), span(j)] = jnp.dot(
                scaled_t[span(i), early], scaled[early, span(j)], preferred_element_type=f32
            )
    wait_obs(2)

    state_copies = []
    for q in range(len(STATE_CUTS) - 1):
        low, high = STATE_CUTS[q], STATE_CUTS[q + 1]
        for n, (dz, dk) in enumerate(hops[:-2] + hops[-1:]):
            to_m = member(dz, dk)
            copy = pltpu.make_async_remote_copy(
                src_ref=states_out.at[to_m, pl.ds(low, high - low)],
                dst_ref=states.at[m, pl.ds(low, high - low)],
                send_sem=state_send.at[q * N_MEM + n],
                recv_sem=state_recv.at[q * N_MEM + m],
                device_id={"mem": to_m, "col": c},
                device_id_type=MESH,
            )
            copy.start()
            state_copies.append(copy)

    def wait_states(q):
        low, high = STATE_CUTS[q], STATE_CUTS[q + 1]
        for dz, dk in hops[:-2] + hops[-1:]:
            source = member(dz, dk)
            pltpu.make_async_remote_copy(
                src_ref=states_out.at[source, pl.ds(low, high - low)],
                dst_ref=states.at[source, pl.ds(low, high - low)],
                send_sem=state_send.at[0],
                recv_sem=state_recv.at[q * N_MEM + source],
                device_id={"mem": source, "col": c},
                device_id_type=MESH,
            ).wait_recv()

    prepare(2)
    squares = jnp.zeros((1, B), f32)
    for j in range(NB):
        for i in range(j + 1):
            tile = cross[span(i), span(j)] + jnp.dot(
                scaled_t[span(i), late], scaled[late, span(j)], preferred_element_type=f32
            )
            cross[span(i), span(j)] = tile
            square = jnp.sum(tile * tile, axis=0, keepdims=True)
            squares = squares + (square if i == j else 2.0 * square)
    bound = (K - 1.0) + jnp.sqrt(jnp.sum(squares, axis=1, keepdims=True))
    inverse_bound = 1.0 / bound
    for j in range(NB):
        for i in range(j + 1):
            tile = cross[span(i), span(j)]
            if i == j:
                tile = tile + (K - 1.0) * unit_block()
            tile = (tile * inverse_bound).astype(bf16)
            put_pair(root_a, i, j, tile)
            put_pair(inverse_a, i, j, halved(tile.astype(f32), i == j).astype(bf16))
    projected = jnp.dot(drive[...], scaled[...], preferred_element_type=f32)

    symmetric_dot(root_a, inverse_a, root_b)
    root, spare_root, inverse, spare_inverse = root_b, root_a, inverse_a, inverse_b
    for sweep in range(1, NS_ITERS):
        symmetric_dot(inverse, root, factor, as_factor=True)
        symmetric_dot(factor, inverse, spare_inverse)
        if sweep + 1 < NS_ITERS:
            symmetric_dot(root, factor, spare_root)
        root, spare_root = spare_root, root
        inverse, spare_inverse = spare_inverse, inverse

    half_step = precise_row_times(projected, inverse)
    mean_w = precise_row_times(half_step, inverse) * inverse_bound
    scale = jnp.sqrt((K - 1.0) * inverse_bound)
    weights = factor
    for i in range(N_MEM):
        part = slice(i * LANES, (i + 1) * LANES)
        column = jnp.broadcast_to(mean_w[:1, part], (LANES, LANES)).T
        for j in range(N_MEM):
            other = slice(j * LANES, (j + 1) * LANES)
            weights[part, other] = (scale * inverse[part, other].astype(f32) + column).astype(bf16)

    out_copies = []
    for q in range(len(STATE_CUTS) - 1):
        low, high = STATE_CUTS[q], STATE_CUTS[q + 1]
        wait_states(q)
        total = states[0, low:high, :].astype(f32)
        for source in range(1, N_MEM):
            total = total + states[source, low:high, :].astype(f32)
        mean = jnp.sum(total, axis=1, keepdims=True) * (1.0 / K)
        for source in range(N_MEM):
            columns = slice(source * LANES, (source + 1) * LANES)
            spread[low:high, columns] = (states[source, low:high, :].astype(f32) - mean).astype(bf16)
        for j in range(NB):
            product = jnp.dot(spread[low:high, :], weights[:, span(j)], preferred_element_type=f32)
            result[low:high, span(j)] = (mean + product).astype(bf16)
        cut = pl.ds(low, high - low)
        copy = pltpu.make_async_copy(result.at[cut], out_hbm.at[cut], out_sem.at[q])
        copy.start()
        out_copies.append(copy)
    for copy in out_copies:
        copy.wait()
    for copy in obs_copies + state_copies:
        copy.wait_send()


def body(
    prior_trajectory,
    predicted_measurements,
    departure_vector,
    measurement_error_spread,
    valid_tallies,
    area_point_sequence,
    nearby_batch_map,
):
    anywhere = pl.BlockSpec(memory_space=pl.ANY)
    scalars = pl.BlockSpec(memory_space=pltpu.SMEM)
    matrix = pltpu.VMEM((K, K), bf16)
    partners = 3 * N_MEM - 1
    cuts = len(STATE_CUTS) - 1
    result = pl.pallas_call(
        kernel,
        out_shape=jax.ShapeDtypeStruct((STATE_ROWS, K), bf16),
        in_specs=[anywhere] * 4 + [scalars] * 3,
        out_specs=anywhere,
        scratch_shapes=[
            pltpu.VMEM((LAYERS, SLAB, LANES), bf16),
            pltpu.VMEM((OBR, BLK, LANES), bf16),
            pltpu.VMEM((3, OBR, BLK), f32),
            pltpu.VMEM((3, OBR, BLK), f32),
            pltpu.VMEM((partners, SLOT_ROWS, LANES), bf16),
            pltpu.VMEM((N_MEM, OBS_ROWS, LANES), bf16),
            pltpu.VMEM((N_MEM, STATE_ROWS, LANES), bf16),
            pltpu.VMEM((N_MEM, STATE_ROWS, LANES), bf16),
            pltpu.VMEM((OBS_ROWS, K), bf16),
            pltpu.VMEM((K, OBS_ROWS), bf16),
            pltpu.VMEM((K, K), f32),
            matrix, matrix, matrix, matrix, matrix,
            pltpu.VMEM((STATE_ROWS, K), bf16),
            pltpu.VMEM((STATE_ROWS, K), bf16),
            pltpu.VMEM((2 * SLAB, 2 * SLAB), f32),
            pltpu.VMEM((16, OBS_ROWS), bf16),
            pltpu.SemaphoreType.DMA((LOADS + 7,)),
            pltpu.SemaphoreType.DMA((partners,)),
            pltpu.SemaphoreType.DMA((3 * N_MEM,)),
            pltpu.SemaphoreType.DMA((cuts * N_MEM,)),
            pltpu.SemaphoreType.DMA((cuts * N_MEM,)),
            pltpu.SemaphoreType.DMA((cuts,)),
        ],
        compiler_params=pltpu.CompilerParams(
            collective_id=0, has_side_effects=True, vmem_limit_bytes=56 * 2**20
        ),
        cost_estimate=pl.CostEstimate(flops=32 * 10**9, bytes_accessed=16 * 10**6, transcendentals=0),
    )(
        prior_trajectory,
        predicted_measurements,
        departure_vector,
        measurement_error_spread,
        valid_tallies,
        area_point_sequence,
        jnp.transpose(nearby_batch_map, (1, 2, 0)),
    )
    return result.reshape(LAYERS, CD, K)


def solution(mesh):
    in_specs = (P(None, "col", "mem"), P("col", None, "mem"), P(), P(), P(), P("col"), P())
    out_specs = P(None, ("mem", "col"), None)
    return jax.shard_map(body, mesh=mesh, in_specs=in_specs, out_specs=out_specs, check_vma=False)
```

```python
import functools

import jax
import jax.numpy as jnp
from jax import lax
from jax.experimental import pallas as pl
from jax.experimental.pallas import tpu as pltpu
from jax.sharding import PartitionSpec as P

NS_ITERS = 5
N_MEM, N_COL = 8, 16
K = 1024
LAYERS, CD, SLAB = 94, 8, 64
STATE_ROWS = LAYERS * CD
OBR, BLK, NPER = 256, 128, 3
SLOT_ROWS = NPER * BLK
OBS_ROWS = 3 * SLOT_ROWS
LANES = K // N_MEM
B = 256
NB = K // B
LOADS = 8
STATE_CUTS = (0, 256, 512, 752)
MESH = pl.DeviceIdType.MESH
f32, bf16 = jnp.float32, jnp.bfloat16


def unit_block():
    row = lax.broadcasted_iota(jnp.int32, (B, B), 0)
    column = lax.broadcasted_iota(jnp.int32, (B, B), 1)
    return jnp.where(row == column, 1.0, 0.0).astype(f32)


def span(i):
    return slice(i * B, (i + 1) * B)


def put_pair(dst, i, j, tile):
    dst[span(i), span(j)] = tile
    if i != j:
        dst[span(j), span(i)] = tile.T


def halved(tile, diagonal):
    return (3.0 * unit_block() - tile) * 0.5 if diagonal else tile * -0.5


def symmetric_dot(a, b, dst, as_factor=False, beside=()):
    steps = list(beside)
    share = -(-len(steps) // (NB * (NB + 1) // 2))
    for j in range(NB):
        for i in range(j + 1):
            tile = jnp.dot(a[span(i), :], b[:, span(j)], preferred_element_type=f32)
            if as_factor:
                tile = halved(tile, i == j)
            put_pair(dst, i, j, tile.astype(bf16))
            for step in steps[:share]:
                step()
            steps = steps[share:]


def precise_row_times(row, matrix):
    high = row.astype(bf16).astype(f32)
    middle = (row - high).astype(bf16).astype(f32)
    low = row - high - middle
    place = lax.broadcasted_iota(jnp.int32, row.shape, 0)
    terms = jnp.where(place == 0, high, jnp.where(place == 1, middle, jnp.where(place == 2, low, 0.0)))
    product = jnp.dot(terms.astype(bf16), matrix[...], preferred_element_type=f32)
    return jnp.broadcast_to(jnp.sum(product, axis=0, keepdims=True), product.shape)


def kernel(
    prior_hbm, obs_hbm, departure_hbm, variance_hbm, counts, sequence, nearby, out_hbm,
    prior, obs, departure, variance, outgoing, rows, states_out, states, scaled, scaled_t,
    cross, root_a, root_b, inverse_a, inverse_b, factor, spread, state_mean, result, pick, drive,
    load_sem, obs_send, obs_recv, state_send, state_recv, out_sem,
):
    m = lax.axis_index("mem")
    c = lax.axis_index("col")

    def column_of(s):
        return lax.rem(c - s + 1 + N_COL, N_COL)

    def member(dz, dk):
        return lax.rem(m // 2 + dz, 4) * 2 + lax.rem(lax.rem(m, 2) + dk, 2)

    hops = [(dz, dk) for dz in (1, 3, 2, 0) for dk in (0, 1)]
    partners = [(s, dz, dk) for dz, dk in hops for s in (1, 0, 2) if (s, dz, dk) != (1, 0, 0)]

    loads = []
    part = OBR // LOADS
    for i in range(LOADS):
        cut = pl.ds(i * part, part)
        loads.append(pltpu.make_async_copy(obs_hbm.at[cut], obs.at[cut], load_sem.at[i]))
    for s in range(3):
        region = lax.rem(c + s - 1 + N_COL, N_COL)
        cut = pl.ds(pl.multiple_of(region * OBR, OBR), OBR)
        loads.append(pltpu.make_async_copy(departure_hbm.at[cut], departure.at[s], load_sem.at[LOADS + 2 * s]))
        loads.append(pltpu.make_async_copy(variance_hbm.at[cut], variance.at[s], load_sem.at[LOADS + 2 * s + 1]))
    loads.append(pltpu.make_async_copy(prior_hbm, prior, load_sem.at[LOADS + 6]))
    for copy in loads[:LOADS]:
        copy.start()

    barrier = pltpu.get_barrier_semaphore()
    for s, dz, dk in partners:
        pl.semaphore_signal(
            barrier, inc=1, device_id={"mem": member(dz, dk), "col": column_of(s)}, device_id_type=MESH
        )

    for copy in loads[:LOADS]:
        copy.wait()
    for copy in loads[LOADS:]:
        copy.start()

    def block_index(group_m, group_c, s, k):
        return nearby[s, k, group_m * N_COL + group_c]

    for k in range(NPER):
        at = SLOT_ROWS + k * BLK
        rows[m, at : at + BLK, :] = obs[block_index(m, c, 1, k)]
    pl.semaphore_wait(barrier, len(partners))
    obs_copies = []
    for n, (s, dz, dk) in enumerate(partners):
        to_m, to_c = member(dz, dk), column_of(s)
        for k in range(NPER):
            outgoing[n, k * BLK : (k + 1) * BLK, :] = obs[block_index(to_m, to_c, s, k)]
        copy = pltpu.make_async_remote_copy(
            src_ref=outgoing.at[n],
            dst_ref=rows.at[m, pl.ds(s * SLOT_ROWS, SLOT_ROWS)],
            send_sem=obs_send.at[n],
            recv_sem=obs_recv.at[s * N_MEM + m],
            device_id={"mem": to_m, "col": to_c},
            device_id_type=MESH,
        )
        copy.start()
        obs_copies.append(copy)

    def wait_obs(s):
        for dz, dk in hops:
            if (s, dz, dk) != (1, 0, 0):
                source = member(dz, dk)
                pltpu.make_async_remote_copy(
                    src_ref=outgoing.at[0],
                    dst_ref=rows.at[source, pl.ds(s * SLOT_ROWS, SLOT_ROWS)],
                    send_sem=obs_send.at[0],
                    recv_sem=obs_recv.at[s * N_MEM + source],
                    device_id={"mem": source, "col": c},
                    device_id_type=MESH,
                ).wait_recv()

    for copy in loads[LOADS:]:
        copy.wait()
    place = lax.broadcasted_iota(jnp.int32, (1, 2 * SLAB), 1)
    for owner in range(N_MEM):
        for j in range(CD):
            column = sequence[owner * CD + j]
            for layer in range(2):
                r = owner * 2 * CD + layer * CD + j
                pick[r : r + 1, :] = jnp.where(place == column + layer * SLAB, 1.0, 0.0).astype(f32)
    picker = pick[...].astype(bf16)

    @pl.loop(0, LAYERS // 2)
    def _(p):
        pair = prior[pl.ds(p * 2, 2)].reshape(2 * SLAB, LANES)
        chosen = jnp.dot(picker, pair, preferred_element_type=f32).astype(bf16)
        at = pl.ds(pl.multiple_of(p * 2 * CD, 2 * CD), 2 * CD)
        for owner in range(N_MEM):
            states_out[owner, at, :] = chosen[owner * 2 * CD : (owner + 1) * 2 * CD]

    states[m] = states_out[m]

    lane = lax.broadcasted_iota(jnp.int32, (1, BLK), 1)

    def prepare(s):
        for k in range(NPER):
            at = s * SLOT_ROWS + k * BLK
            index = block_index(m, c, s, k)
            region = lax.rem(c + s - 1 + N_COL, N_COL)
            count = counts[region * OBR + index]
            row_w = jnp.where(lane < count, 1.0, 0.0) * lax.rsqrt(variance[s, pl.ds(index, 1), :])
            driven = (departure[s, pl.ds(index, 1), :] * row_w).astype(bf16)
            drive[:, at : at + BLK] = jnp.broadcast_to(driven, (16, BLK))
            column_w = jnp.broadcast_to(row_w, (BLK, BLK)).T
            total = rows[0, at : at + BLK, :].astype(f32)
            for source in range(1, N_MEM):
                total = total + rows[source, at : at + BLK, :].astype(f32)
            mean = jnp.sum(total, axis=1, keepdims=True) * (1.0 / K)
            for source in range(N_MEM):
                tile = ((rows[source, at : at + BLK, :].astype(f32) - mean) * column_w).astype(bf16)
                columns = slice(source * LANES, (source + 1) * LANES)
                scaled[at : at + BLK, columns] = tile
                scaled_t[columns, at : at + BLK] = tile.T

    early, late = slice(0, 2 * SLOT_ROWS), slice(2 * SLOT_ROWS, OBS_ROWS)
    wait_obs(1)
    state_copies = []
    for q in range(len(STATE_CUTS) - 1):
        low, high = STATE_CUTS[q], STATE_CUTS[q + 1]
        for n, (dz, dk) in enumerate(hops[:-2] + hops[-1:]):
            to_m = member(dz, dk)
            copy = pltpu.make_async_remote_copy(
                src_ref=states_out.at[to_m, pl.ds(low, high - low)],
                dst_ref=states.at[m, pl.ds(low, high - low)],
                send_sem=state_send.at[q * N_MEM + n],
                recv_sem=state_recv.at[q * N_MEM + m],
                device_id={"mem": to_m, "col": c},
                device_id_type=MESH,
            )
            copy.start()
            state_copies.append(copy)

    prepare(1)
    wait_obs(0)
    prepare(0)
    for j in range(NB):
        for i in range(j + 1):
            cross[span(i), span(j)] = jnp.dot(
                scaled_t[span(i), early], scaled[early, span(j)], preferred_element_type=f32
            )
    wait_obs(2)

    def wait_states(q):
        low, high = STATE_CUTS[q], STATE_CUTS[q + 1]
        for dz, dk in hops[:-2] + hops[-1:]:
            source = member(dz, dk)
            pltpu.make_async_remote_copy(
                src_ref=states_out.at[source, pl.ds(low, high - low)],
                dst_ref=states.at[source, pl.ds(low, high - low)],
                send_sem=state_send.at[0],
                recv_sem=state_recv.at[q * N_MEM + source],
                device_id={"mem": source, "col": c},
                device_id_type=MESH,
            ).wait_recv()

    def centre(low, high):
        total = states[0, low:high, :].astype(f32)
        for source in range(1, N_MEM):
            total = total + states[source, low:high, :].astype(f32)
        mean = jnp.sum(total, axis=1, keepdims=True) * (1.0 / K)
        state_mean[low:high, :] = jnp.broadcast_to(mean, (high - low, LANES))
        for source in range(N_MEM):
            columns = slice(source * LANES, (source + 1) * LANES)
            spread[low:high, columns] = (states[source, low:high, :].astype(f32) - mean).astype(bf16)

    def centring(q):
        wait_states(q)
        low, high = STATE_CUTS[q], STATE_CUTS[q + 1]
        return [functools.partial(centre, at, at + 16) for at in range(low, high, 16)]

    prepare(2)
    squares = jnp.zeros((1, B), f32)
    for j in range(NB):
        for i in range(j + 1):
            tile = cross[span(i), span(j)] + jnp.dot(
                scaled_t[span(i), late], scaled[late, span(j)], preferred_element_type=f32
            )
            cross[span(i), span(j)] = tile
            square = jnp.sum(tile * tile, axis=0, keepdims=True)
            squares = squares + (square if i == j else 2.0 * square)
    bound = (K - 1.0) + jnp.sqrt(jnp.sum(squares, axis=1, keepdims=True))
    inverse_bound = 1.0 / bound
    for j in range(NB):
        for i in range(j + 1):
            tile = cross[span(i), span(j)]
            if i == j:
                tile = tile + (K - 1.0) * unit_block()
            tile = (tile * inverse_bound).astype(bf16)
            put_pair(root_a, i, j, tile)
            put_pair(inverse_a, i, j, halved(tile.astype(f32), i == j).astype(bf16))
    projected = jnp.dot(drive[...], scaled[...], preferred_element_type=f32)

    symmetric_dot(root_a, inverse_a, root_b)
    root, spare_root, inverse, spare_inverse = root_b, root_a, inverse_a, inverse_b
    for sweep in range(1, NS_ITERS):
        last = sweep + 1 == NS_ITERS
        symmetric_dot(inverse, root, factor, as_factor=True)
        symmetric_dot(factor, inverse, spare_inverse)
        if sweep + 1 < NS_ITERS:
            symmetric_dot(root, factor, spare_root)
        root, spare_root = spare_root, root
        inverse, spare_inverse = spare_inverse, inverse

    half_step = precise_row_times(projected, inverse)
    mean_w = precise_row_times(half_step, inverse) * inverse_bound
    scale = jnp.sqrt((K - 1.0) * inverse_bound)
    weights = factor
    mean_columns = []
    for i in range(N_MEM):
        part = slice(i * LANES, (i + 1) * LANES)
        mean_columns.append(jnp.broadcast_to(mean_w[:1, part], (LANES, LANES)).T)
    out_copies = []
    for q in range(len(STATE_CUTS) - 1):
        low, high = STATE_CUTS[q], STATE_CUTS[q + 1]
        wait_states(q)
        centre(low, high)
        for j in range(NB):
            if q == 0:
                for i in range(N_MEM):
                    part = slice(i * LANES, (i + 1) * LANES)
                    column = jnp.concatenate([mean_columns[i]] * (B // LANES), axis=1)
                    weights[part, span(j)] = (scale * inverse[part, span(j)].astype(f32) + column).astype(bf16)
            product = jnp.dot(spread[low:high, :], weights[:, span(j)], preferred_element_type=f32)
            mean = jnp.concatenate([state_mean[low:high, :]] * (B // LANES), axis=1)
            result[low:high, span(j)] = (mean + product).astype(bf16)
        cut = pl.ds(low, high - low)
        copy = pltpu.make_async_copy(result.at[cut], out_hbm.at[cut], out_sem.at[q])
        copy.start()
        out_copies.append(copy)
    for copy in out_copies:
        copy.wait()
    for copy in obs_copies + state_copies:
        copy.wait_send()


def pin(x):
    return pltpu.with_memory_space_constraint(x, pltpu.HBM)


def body(
    prior_trajectory,
    predicted_measurements,
    departure_vector,
    measurement_error_spread,
    valid_tallies,
    area_point_sequence,
    nearby_batch_map,
):
    anywhere = pl.BlockSpec(memory_space=pl.ANY)
    in_hbm = pl.BlockSpec(memory_space=pltpu.HBM)
    scalars = pl.BlockSpec(memory_space=pltpu.SMEM)
    matrix = pltpu.VMEM((K, K), bf16)
    partners = 3 * N_MEM - 1
    cuts = len(STATE_CUTS) - 1
    result = pl.pallas_call(
        kernel,
        out_shape=jax.ShapeDtypeStruct((STATE_ROWS, K), bf16),
        in_specs=[in_hbm] * 4 + [scalars] * 3,
        out_specs=anywhere,
        scratch_shapes=[
            pltpu.VMEM((LAYERS, SLAB, LANES), bf16),
            pltpu.VMEM((OBR, BLK, LANES), bf16),
            pltpu.VMEM((3, OBR, BLK), f32),
            pltpu.VMEM((3, OBR, BLK), f32),
            pltpu.VMEM((partners, SLOT_ROWS, LANES), bf16),
            pltpu.VMEM((N_MEM, OBS_ROWS, LANES), bf16),
            pltpu.VMEM((N_MEM, STATE_ROWS, LANES), bf16),
            pltpu.VMEM((N_MEM, STATE_ROWS, LANES), bf16),
            pltpu.VMEM((OBS_ROWS, K), bf16),
            pltpu.VMEM((K, OBS_ROWS), bf16),
            pltpu.VMEM((K, K), f32),
            matrix, matrix, matrix, matrix, matrix,
            pltpu.VMEM((STATE_ROWS, K), bf16),
            pltpu.VMEM((STATE_ROWS, LANES), f32),
            pltpu.VMEM((STATE_ROWS, K), bf16),
            pltpu.VMEM((2 * SLAB, 2 * SLAB), f32),
            pltpu.VMEM((16, OBS_ROWS), bf16),
            pltpu.SemaphoreType.DMA((LOADS + 7,)),
            pltpu.SemaphoreType.DMA((partners,)),
            pltpu.SemaphoreType.DMA((3 * N_MEM,)),
            pltpu.SemaphoreType.DMA((cuts * N_MEM,)),
            pltpu.SemaphoreType.DMA((cuts * N_MEM,)),
            pltpu.SemaphoreType.DMA((cuts,)),
        ],
        compiler_params=pltpu.CompilerParams(
            collective_id=0, has_side_effects=True, vmem_limit_bytes=48 * 2**20
        ),
        cost_estimate=pl.CostEstimate(flops=32 * 10**9, bytes_accessed=16 * 10**6, transcendentals=0),
    )(
        pin(prior_trajectory),
        pin(predicted_measurements),
        pin(departure_vector),
        pin(measurement_error_spread),
        pin(valid_tallies),
        pin(area_point_sequence),
        pin(jnp.transpose(nearby_batch_map, (1, 2, 0))),
    )
    return result.reshape(LAYERS, CD, K)


def solution(mesh):
    in_specs = (P(None, "col", "mem"), P("col", None, "mem"), P(), P(), P(), P("col"), P())
    out_specs = P(None, ("mem", "col"), None)
    return jax.shard_map(body, mesh=mesh, in_specs=in_specs, out_specs=out_specs, check_vma=False)
```

```python
import jax
import jax.numpy as jnp
from jax import lax
from jax.experimental import pallas as pl
from jax.experimental.pallas import tpu as pltpu
from jax.sharding import PartitionSpec as P

NS_ITERS = 5
N_MEM, N_COL = 8, 16
K = 1024
LAYERS, CD, SLAB = 94, 8, 64
STATE_ROWS = LAYERS * CD
OBR, BLK, NPER = 256, 128, 3
SLOT_ROWS = NPER * BLK
OBS_ROWS = 3 * SLOT_ROWS
LANES = K // N_MEM
B = 256
NB = K // B
LOADS = 8
STATE_CUTS = (0, 256, 512, 752)
MESH = pl.DeviceIdType.MESH
f32, bf16 = jnp.float32, jnp.bfloat16


def unit_block():
    row = lax.broadcasted_iota(jnp.int32, (B, B), 0)
    column = lax.broadcasted_iota(jnp.int32, (B, B), 1)
    return jnp.where(row == column, 1.0, 0.0).astype(f32)


def span(i):
    return slice(i * B, (i + 1) * B)


def put_pair(dst, i, j, tile):
    dst[span(i), span(j)] = tile
    if i != j:
        dst[span(j), span(i)] = tile.T


def halved(tile, diagonal):
    return (3.0 * unit_block() - tile) * 0.5 if diagonal else tile * -0.5


def symmetric_dot(a, b, dst, as_factor=False, beside=()):
    steps = list(beside)
    share = -(-len(steps) // (NB * (NB + 1) // 2))
    for j in range(NB):
        for i in range(j + 1):
            tile = jnp.dot(a[span(i), :], b[:, span(j)], preferred_element_type=f32)
            if as_factor:
                tile = halved(tile, i == j)
            put_pair(dst, i, j, tile.astype(bf16))
            for step in steps[:share]:
                step()
            steps = steps[share:]


def precise_row_times(row, matrix):
    high = row.astype(bf16).astype(f32)
    middle = (row - high).astype(bf16).astype(f32)
    low = row - high - middle
    place = lax.broadcasted_iota(jnp.int32, row.shape, 0)
    terms = jnp.where(place == 0, high, jnp.where(place == 1, middle, jnp.where(place == 2, low, 0.0)))
    product = jnp.dot(terms.astype(bf16), matrix[...], preferred_element_type=f32)
    return jnp.broadcast_to(jnp.sum(product, axis=0, keepdims=True), product.shape)


def kernel(
    prior_hbm, obs_hbm, departure_hbm, variance_hbm, counts, sequence, nearby, out_hbm,
    prior, obs, departure, variance, outgoing, rows, states_out, states, scaled, scaled_t,
    cross, root_a, root_b, inverse_a, inverse_b, factor, spread, state_mean, result, pick, drive,
    load_sem, obs_send, obs_recv, state_send, state_recv, out_sem,
):
    m = lax.axis_index("mem")
    c = lax.axis_index("col")

    def column_of(s):
        return lax.rem(c - s + 1 + N_COL, N_COL)

    def member(dz, dk):
        return lax.rem(m // 2 + dz, 4) * 2 + lax.rem(lax.rem(m, 2) + dk, 2)

    hops = [(dz, dk) for dz in (1, 3, 2, 0) for dk in (0, 1)]
    partners = [(s, dz, dk) for dz, dk in hops for s in (1, 0, 2) if (s, dz, dk) != (1, 0, 0)]

    loads = []
    part = OBR // LOADS
    for i in range(LOADS):
        cut = pl.ds(i * part, part)
        loads.append(pltpu.make_async_copy(obs_hbm.at[cut], obs.at[cut], load_sem.at[i]))
    for s in range(3):
        region = lax.rem(c + s - 1 + N_COL, N_COL)
        cut = pl.ds(pl.multiple_of(region * OBR, OBR), OBR)
        loads.append(pltpu.make_async_copy(departure_hbm.at[cut], departure.at[s], load_sem.at[LOADS + 2 * s]))
        loads.append(pltpu.make_async_copy(variance_hbm.at[cut], variance.at[s], load_sem.at[LOADS + 2 * s + 1]))
    loads.append(pltpu.make_async_copy(prior_hbm, prior, load_sem.at[LOADS + 6]))
    for copy in loads[:LOADS]:
        copy.start()

    barrier = pltpu.get_barrier_semaphore()
    for s, dz, dk in partners:
        pl.semaphore_signal(
            barrier, inc=1, device_id={"mem": member(dz, dk), "col": column_of(s)}, device_id_type=MESH
        )

    for copy in loads[:LOADS]:
        copy.wait()
    for copy in loads[LOADS:]:
        copy.start()

    def block_index(group_m, group_c, s, k):
        return nearby[s, k, group_m * N_COL + group_c]

    for k in range(NPER):
        at = SLOT_ROWS + k * BLK
        rows[m, at : at + BLK, :] = obs[block_index(m, c, 1, k)]
    pl.semaphore_wait(barrier, len(partners))
    obs_copies = []
    for n, (s, dz, dk) in enumerate(partners):
        to_m, to_c = member(dz, dk), column_of(s)
        for k in range(NPER):
            outgoing[n, k * BLK : (k + 1) * BLK, :] = obs[block_index(to_m, to_c, s, k)]
        copy = pltpu.make_async_remote_copy(
            src_ref=outgoing.at[n],
            dst_ref=rows.at[m, pl.ds(s * SLOT_ROWS, SLOT_ROWS)],
            send_sem=obs_send.at[n],
            recv_sem=obs_recv.at[s * N_MEM + m],
            device_id={"mem": to_m, "col": to_c},
            device_id_type=MESH,
        )
        copy.start()
        obs_copies.append(copy)

    def wait_obs(s):
        for dz, dk in hops:
            if (s, dz, dk) != (1, 0, 0):
                source = member(dz, dk)
                pltpu.make_async_remote_copy(
                    src_ref=outgoing.at[0],
                    dst_ref=rows.at[source, pl.ds(s * SLOT_ROWS, SLOT_ROWS)],
                    send_sem=obs_send.at[0],
                    recv_sem=obs_recv.at[s * N_MEM + source],
                    device_id={"mem": source, "col": c},
                    device_id_type=MESH,
                ).wait_recv()

    for copy in loads[LOADS:]:
        copy.wait()
    place = lax.broadcasted_iota(jnp.int32, (1, 2 * SLAB), 1)
    for owner in range(N_MEM):
        for j in range(CD):
            column = sequence[owner * CD + j]
            for layer in range(2):
                r = owner * 2 * CD + layer * CD + j
                pick[r : r + 1, :] = jnp.where(place == column + layer * SLAB, 1.0, 0.0).astype(f32)
    picker = pick[...].astype(bf16)

    @pl.loop(0, LAYERS // 2)
    def _(p):
        pair = prior[pl.ds(p * 2, 2)].reshape(2 * SLAB, LANES)
        chosen = jnp.dot(picker, pair, preferred_element_type=f32).astype(bf16)
        at = pl.ds(pl.multiple_of(p * 2 * CD, 2 * CD), 2 * CD)
        for owner in range(N_MEM):
            states_out[owner, at, :] = chosen[owner * 2 * CD : (owner + 1) * 2 * CD]

    states[m] = states_out[m]

    lane = lax.broadcasted_iota(jnp.int32, (1, BLK), 1)

    def prepare(s):
        for k in range(NPER):
            at = s * SLOT_ROWS + k * BLK
            index = block_index(m, c, s, k)
            region = lax.rem(c + s - 1 + N_COL, N_COL)
            count = counts[region * OBR + index]
            row_w = jnp.where(lane < count, 1.0, 0.0) * lax.rsqrt(variance[s, pl.ds(index, 1), :])
            driven = (departure[s, pl.ds(index, 1), :] * row_w).astype(bf16)
            drive[:, at : at + BLK] = jnp.broadcast_to(driven, (16, BLK))
            column_w = jnp.broadcast_to(row_w, (BLK, BLK)).T
            total = rows[0, at : at + BLK, :].astype(f32)
            for source in range(1, N_MEM):
                total = total + rows[source, at : at + BLK, :].astype(f32)
            mean = jnp.sum(total, axis=1, keepdims=True) * (1.0 / K)
            for source in range(N_MEM):
                tile = ((rows[source, at : at + BLK, :].astype(f32) - mean) * column_w).astype(bf16)
                columns = slice(source * LANES, (source + 1) * LANES)
                scaled[at : at + BLK, columns] = tile
                scaled_t[columns, at : at + BLK] = tile.T

    for copy in obs_copies[:12]:
        copy.wait_send()
    state_copies = []
    for q in range(len(STATE_CUTS) - 1):
        low, high = STATE_CUTS[q], STATE_CUTS[q + 1]
        for n, (dz, dk) in enumerate(hops[:-2] + hops[-1:]):
            to_m = member(dz, dk)
            copy = pltpu.make_async_remote_copy(
                src_ref=states_out.at[to_m, pl.ds(low, high - low)],
                dst_ref=states.at[m, pl.ds(low, high - low)],
                send_sem=state_send.at[q * N_MEM + n],
                recv_sem=state_recv.at[q * N_MEM + m],
                device_id={"mem": to_m, "col": c},
                device_id_type=MESH,
            )
            copy.start()
            state_copies.append(copy)

    wait_obs(1)
    prepare(1)
    wait_obs(0)
    prepare(0)
    wait_obs(2)

    def wait_states(q):
        low, high = STATE_CUTS[q], STATE_CUTS[q + 1]
        for dz, dk in hops[:-2] + hops[-1:]:
            source = member(dz, dk)
            pltpu.make_async_remote_copy(
                src_ref=states_out.at[source, pl.ds(low, high - low)],
                dst_ref=states.at[source, pl.ds(low, high - low)],
                send_sem=state_send.at[0],
                recv_sem=state_recv.at[q * N_MEM + source],
                device_id={"mem": source, "col": c},
                device_id_type=MESH,
            ).wait_recv()

    def centre(low, high):
        total = states[0, low:high, :].astype(f32)
        for source in range(1, N_MEM):
            total = total + states[source, low:high, :].astype(f32)
        mean = jnp.sum(total, axis=1, keepdims=True) * (1.0 / K)
        state_mean[low:high, :] = jnp.broadcast_to(mean, (high - low, LANES))
        for source in range(N_MEM):
            columns = slice(source * LANES, (source + 1) * LANES)
            spread[low:high, columns] = (states[source, low:high, :].astype(f32) - mean).astype(bf16)

    prepare(2)
    squares = jnp.zeros((1, B), f32)
    for j in range(NB):
        for i in range(j + 1):
            tile = jnp.dot(scaled_t[span(i), :], scaled[:, span(j)], preferred_element_type=f32)
            cross[span(i), span(j)] = tile
            square = jnp.sum(tile * tile, axis=0, keepdims=True)
            squares = squares + (square if i == j else 2.0 * square)
    bound = (K - 1.0) + jnp.sqrt(jnp.sum(squares, axis=1, keepdims=True))
    inverse_bound = 1.0 / bound
    for j in range(NB):
        for i in range(j + 1):
            tile = cross[span(i), span(j)]
            if i == j:
                tile = tile + (K - 1.0) * unit_block()
            tile = (tile * inverse_bound).astype(bf16)
            put_pair(root_a, i, j, tile)
            put_pair(inverse_a, i, j, halved(tile.astype(f32), i == j).astype(bf16))
    projected = jnp.dot(drive[...], scaled[...], preferred_element_type=f32)

    symmetric_dot(root_a, inverse_a, root_b)
    root, spare_root, inverse, spare_inverse = root_b, root_a, inverse_a, inverse_b
    for sweep in range(1, NS_ITERS):
        last = sweep + 1 == NS_ITERS
        symmetric_dot(inverse, root, factor, as_factor=True)
        symmetric_dot(factor, inverse, spare_inverse)
        if sweep + 1 < NS_ITERS:
            symmetric_dot(root, factor, spare_root)
        root, spare_root = spare_root, root
        inverse, spare_inverse = spare_inverse, inverse

    half_step = precise_row_times(projected, inverse)
    mean_w = precise_row_times(half_step, inverse) * inverse_bound
    scale = jnp.sqrt((K - 1.0) * inverse_bound)
    weights = factor
    mean_columns = []
    for i in range(N_MEM):
        part = slice(i * LANES, (i + 1) * LANES)
        mean_columns.append(jnp.broadcast_to(mean_w[:1, part], (LANES, LANES)).T)
    out_copies = []
    for q in range(len(STATE_CUTS) - 1):
        low, high = STATE_CUTS[q], STATE_CUTS[q + 1]
        if q == 0:
            wait_states(0)
            centre(low, high)
        following = []
        if q + 2 < len(STATE_CUTS):
            wait_states(q + 1)
            end = STATE_CUTS[q + 2]
            following = [(at, min(at + 64, end)) for at in range(high, end, 64)]
        for j in range(NB):
            if q == 0:
                for i in range(N_MEM):
                    part = slice(i * LANES, (i + 1) * LANES)
                    column = jnp.concatenate([mean_columns[i]] * (B // LANES), axis=1)
                    weights[part, span(j)] = (scale * inverse[part, span(j)].astype(f32) + column).astype(bf16)
            product = jnp.dot(spread[low:high, :], weights[:, span(j)], preferred_element_type=f32)
            mean = jnp.concatenate([state_mean[low:high, :]] * (B // LANES), axis=1)
            result[low:high, span(j)] = (mean + product).astype(bf16)
            if following:
                centre(*following.pop(0))
        cut = pl.ds(low, high - low)
        copy = pltpu.make_async_copy(result.at[cut], out_hbm.at[cut], out_sem.at[q])
        copy.start()
        out_copies.append(copy)
    for copy in out_copies:
        copy.wait()
    for copy in obs_copies[12:] + state_copies:
        copy.wait_send()


def pin(x):
    return pltpu.with_memory_space_constraint(x, pltpu.HBM)


def body(
    prior_trajectory,
    predicted_measurements,
    departure_vector,
    measurement_error_spread,
    valid_tallies,
    area_point_sequence,
    nearby_batch_map,
):
    anywhere = pl.BlockSpec(memory_space=pl.ANY)
    in_hbm = pl.BlockSpec(memory_space=pltpu.HBM)
    scalars = pl.BlockSpec(memory_space=pltpu.SMEM)
    matrix = pltpu.VMEM((K, K), bf16)
    partners = 3 * N_MEM - 1
    cuts = len(STATE_CUTS) - 1
    result = pl.pallas_call(
        kernel,
        out_shape=jax.ShapeDtypeStruct((STATE_ROWS, K), bf16),
        in_specs=[in_hbm] * 4 + [scalars] * 3,
        out_specs=anywhere,
        scratch_shapes=[
            pltpu.VMEM((LAYERS, SLAB, LANES), bf16),
            pltpu.VMEM((OBR, BLK, LANES), bf16),
            pltpu.VMEM((3, OBR, BLK), f32),
            pltpu.VMEM((3, OBR, BLK), f32),
            pltpu.VMEM((partners, SLOT_ROWS, LANES), bf16),
            pltpu.VMEM((N_MEM, OBS_ROWS, LANES), bf16),
            pltpu.VMEM((N_MEM, STATE_ROWS, LANES), bf16),
            pltpu.VMEM((N_MEM, STATE_ROWS, LANES), bf16),
            pltpu.VMEM((OBS_ROWS, K), bf16),
            pltpu.VMEM((K, OBS_ROWS), bf16),
            pltpu.VMEM((K, K), f32),
            matrix, matrix, matrix, matrix, matrix,
            pltpu.VMEM((STATE_ROWS, K), bf16),
            pltpu.VMEM((STATE_ROWS, LANES), f32),
            pltpu.VMEM((STATE_ROWS, K), bf16),
            pltpu.VMEM((2 * SLAB, 2 * SLAB), f32),
            pltpu.VMEM((16, OBS_ROWS), bf16),
            pltpu.SemaphoreType.DMA((LOADS + 7,)),
            pltpu.SemaphoreType.DMA((partners,)),
            pltpu.SemaphoreType.DMA((3 * N_MEM,)),
            pltpu.SemaphoreType.DMA((cuts * N_MEM,)),
            pltpu.SemaphoreType.DMA((cuts * N_MEM,)),
            pltpu.SemaphoreType.DMA((cuts,)),
        ],
        compiler_params=pltpu.CompilerParams(
            collective_id=0, has_side_effects=True, vmem_limit_bytes=48 * 2**20
        ),
        cost_estimate=pl.CostEstimate(flops=32 * 10**9, bytes_accessed=16 * 10**6, transcendentals=0),
    )(
        pin(prior_trajectory),
        pin(predicted_measurements),
        pin(departure_vector),
        pin(measurement_error_spread),
        pin(valid_tallies),
        pin(area_point_sequence),
        pin(jnp.transpose(nearby_batch_map, (1, 2, 0))),
    )
    return result.reshape(LAYERS, CD, K)


def solution(mesh):
    in_specs = (P(None, "col", "mem"), P("col", None, "mem"), P(), P(), P(), P("col"), P())
    out_specs = P(None, ("mem", "col"), None)
    return jax.shard_map(body, mesh=mesh, in_specs=in_specs, out_specs=out_specs, check_vma=False)
```
